512 devices in a mesh: replica: 4 (over x), fsdp: 16 (over z_lo, y), tensor: 8 (over z_hi, core).
Axes of the slice: x: 4, y: 4, z: 16 (z_hi: 4, z_lo: 4; z = z_hi * 4 + z_lo), core: 2. Of those that a mesh axis runs over, the one named last changes fastest.
Arguments:
- tokens: bfloat16 [4, 4096, 8192], P('replica', 'fsdp', 'tensor'), may hold values from -6 to 6
- queries: bfloat16 [4, 4096, 8192], P('replica', 'fsdp', 'tensor'), may hold values from -68 to 68
- out_grad: bfloat16 [4, 4096, 8192], P('replica', 'fsdp', 'tensor'), may hold values from -6 to 6
- kv_weight: bfloat16 [4, 2, 8192, 1024], P('replica', None, 'fsdp', 'tensor'), may hold values from -0.0625 to 0.0625
- first_moment: bfloat16 [4, 2, 8192, 1024], P('replica', None, 'fsdp', 'tensor'), may hold values from -30 to 30
- second_moment: bfloat16 [4, 2, 8192, 1024], P('replica', None, 'fsdp', 'tensor'), may hold values from 20 to 2000
- pseudo_grads: float32 [4, 8192, 1024], P('replica', 'fsdp', 'tensor'), may hold values from -6 to 6
- outer_momentum: float32 [8192, 1024], P('fsdp', 'tensor'), may hold values from -6 to 6
- anchor: float32 [8192, 1024], P('fsdp', 'tensor'), may hold values from -6 to 6
Outputs:
- new_weight: bfloat16 [4, 2, 8192, 1024], P('replica', None, 'fsdp', 'tensor')
- new_first: bfloat16 [4, 2, 8192, 1024], P('replica', None, 'fsdp', 'tensor')
- new_second: bfloat16 [4, 2, 8192, 1024], P('replica', None, 'fsdp', 'tensor')
- new_anchor: float32 [8192, 1024], P('fsdp', 'tensor')
- new_momentum: float32 [8192, 1024], P('fsdp', 'tensor')
The draws below stay inside these ranges and needn't reach their ends.
All inputs are finite; a program needn't handle non-finite values.
Results may differ from the reference program's by a relative error of at most 0.04.
Values may be sent and summed in bfloat16 or wider, within the bound.
A program may use at most 64 MiB of HBM per device.

```python
import math
import jax
import jax.numpy as jnp
from jax import lax

D = 8192
HD = 128
STEP = 5
TOK_DEV = 256
TOKENS = 4096
REPLICAS = 4
Q_COLS = 8192
KV_COLS = 1024
N_REPLICA = 4
N_FSDP = 16


def draw_queries(key, part):
    key = jax.random.fold_in(key, 7)
    normal_values = jax.random.normal(key, (REPLICAS, TOKENS, Q_COLS), jnp.float32)
    return jnp.clip(normal_values, -6.0, 6.0).astype(jnp.bfloat16)


def steps_of(stream_key, shape, pieces, least, high):
    def one(dim, shards_of):
        heights = jax.random.uniform(jax.random.fold_in(jax.random.fold_in(stream_key, 6), dim), (shards_of,), jnp.float32, least / len(pieces), high / len(pieces))
        return jnp.repeat(jnp.exp(heights), shape[dim] // shards_of).reshape((-1,) + (1,) * (len(shape) - dim - 1))

    level = one(*pieces[0])
    for cut in pieces[1:]:
        level = level * one(*cut)
    return level


def centred(key, shape, width, reach, pieces=(), held_as=jnp.bfloat16):
    entries = width * jax.random.normal(key, shape, jnp.float32)
    if pieces:
        entries = entries * steps_of(key, shape, pieces, -0.22, 0.18)
    return jnp.clip(entries, -reach, reach).astype(held_as)


def setup_inputs(seed: int = 0) -> dict:
    streams_of = jax.random.split(jax.random.key(seed), 10)
    tokens = centred(streams_of[0], (REPLICAS, TOKENS, D), 1.0, 6.0, ((0, 4), (1, 16), (2, 8)))
    queries = draw_queries(jax.random.fold_in(streams_of[9], 71), 0)
    out_grad = centred(streams_of[2], (REPLICAS, TOKENS, Q_COLS), 1.0, 6.0, ((0, 4), (1, 16), (2, 8)))
    kv_weight = centred(streams_of[3], (REPLICAS, 2, D, KV_COLS), D ** -0.5, 0.0625, ((0, 4), (2, 16), (3, 8)))
    first_moment = centred(streams_of[4], (REPLICAS, 2, D, KV_COLS), 5.0, 30.0, ((0, 4), (2, 16), (3, 8)))
    second_moment = jnp.clip(jnp.exp(math.log(2000.0) - 4.6051702 * jax.random.uniform(streams_of[5], (REPLICAS, 2, D, KV_COLS), jnp.float32) ** steps_of(streams_of[5], (REPLICAS, 2, D, KV_COLS), ((0, 4), (2, 16), (3, 8)), -0.2, 0.2)), 20.0, 2000.0).astype(jnp.bfloat16)
    pseudo_grads = centred(streams_of[6], (REPLICAS, D, KV_COLS), 1.0, 6.0, ((0, 4), (1, 16), (2, 8)), jnp.float32)
    outer_momentum = centred(streams_of[7], (D, KV_COLS), 1.0, 6.0, ((0, 16), (1, 8)), jnp.float32)
    anchor = centred(streams_of[8], (D, KV_COLS), 1.0, 6.0, ((0, 16), (1, 8)), jnp.float32)
    return {"tokens": tokens, "queries": queries, "out_grad": out_grad, "kv_weight": kv_weight, "first_moment": first_moment, "second_moment": second_moment, "pseudo_grads": pseudo_grads, "outer_momentum": outer_momentum, "anchor": anchor}


first_decay = 0.9
second_decay = 0.95
inner_rate = 0.001
weight_decay = 0.1
adam_epsilon = 1e-08
outer_rate = 0.7
outer_decay = 0.9

def attention_grads(query_rows, grad_rows, key_rows, value_rows):
    length = key_rows.shape[0]
    kv_heads = key_rows.shape[1] // HD
    members = query_rows.shape[1] // key_rows.shape[1]
    scaling = HD ** (-0.5)
    query_heads = query_rows.reshape(length, kv_heads, members, HD).astype(jnp.float32)
    grad_heads = grad_rows.reshape(length, kv_heads, members, HD).astype(jnp.float32)
    key_heads = key_rows.reshape(length, kv_heads, HD).astype(jnp.float32)
    value_heads = value_rows.reshape(length, kv_heads, HD).astype(jnp.float32)
    scores = jnp.einsum('ihgd,jhd->hgij', query_heads, key_heads) * scaling
    causal = jnp.arange(length)[:, None] >= jnp.arange(length)[None, :]
    scores = jnp.where(causal, scores, -jnp.inf)
    probabilities = jax.nn.softmax(scores, axis=-1)
    rounded_probs = probabilities.astype(jnp.bfloat16).astype(jnp.float32)
    value_grads = jnp.einsum('hgij,ihgd->jhd', rounded_probs, grad_heads)
    prob_grads = jnp.einsum('ihgd,jhd->hgij', grad_heads, value_heads)
    row_delta = lax.optimization_barrier(jnp.sum(probabilities * prob_grads, axis=-1, keepdims=True))
    score_grads = (probabilities * (prob_grads - row_delta) * scaling).astype(jnp.bfloat16).astype(jnp.float32)
    key_grads = jnp.einsum('hgij,ihgd->jhd', score_grads, query_heads)
    joined = jnp.concatenate([key_grads.reshape(length, -1), value_grads.reshape(length, -1)], axis=1)
    return joined.astype(jnp.bfloat16)

def apply_adamw(weights, first_moment, second_moment, gradient):
    first_new = first_decay * first_moment.astype(jnp.float32) + (1.0 - first_decay) * gradient
    second_new = second_decay * second_moment.astype(jnp.float32) + (1.0 - second_decay) * gradient * gradient
    corrected_first = first_new / (1.0 - first_decay ** STEP)
    corrected_second = second_new / (1.0 - second_decay ** STEP)
    current = weights.astype(jnp.float32)
    updated = current - inner_rate * (corrected_first / (jnp.sqrt(corrected_second) + adam_epsilon) + weight_decay * current)
    return (updated.astype(jnp.bfloat16), first_new.astype(jnp.bfloat16), second_new.astype(jnp.bfloat16))

def outer_step(averaged, momentum, anchor):
    momentum_new = outer_decay * momentum + averaged
    anchor_new = anchor - outer_rate * (averaged + outer_decay * momentum_new)
    return (anchor_new, momentum_new)

def one_replica(items):
    token_all, query_all, grad_all, weights, first_in, second_in = items

    def one_block(running, position):
        offset = position * TOK_DEV
        token_rows = lax.dynamic_slice_in_dim(token_all, offset, TOK_DEV, 0)
        query_rows = lax.dynamic_slice_in_dim(query_all, offset, TOK_DEV, 0)
        grad_rows = lax.dynamic_slice_in_dim(grad_all, offset, TOK_DEV, 0)
        key_rows = jnp.dot(token_rows, weights[0], preferred_element_type=jnp.float32).astype(jnp.bfloat16)
        value_rows = jnp.dot(token_rows, weights[1], preferred_element_type=jnp.float32).astype(jnp.bfloat16)
        kv_grads = attention_grads(query_rows, grad_rows, key_rows, value_rows)
        partial_sum = jnp.dot(token_rows.T, kv_grads, preferred_element_type=jnp.float32)
        rounded = lax.optimization_barrier(partial_sum.astype(jnp.bfloat16))
        return (running + rounded.astype(jnp.float32), None)
    initial = jnp.zeros((D, 2 * KV_COLS), jnp.float32)
    summed, _ = lax.scan(one_block, initial, jnp.arange(N_FSDP, dtype=jnp.int32))
    gradient = summed.reshape(D, 2, KV_COLS).transpose(1, 0, 2)
    return apply_adamw(weights, first_in, second_in, gradient)

def reference(tokens, queries, out_grad, kv_weight, first_moment, second_moment, pseudo_grads, outer_momentum, anchor):
    new_weight, new_first, new_second = lax.map(one_replica, (tokens, queries, out_grad, kv_weight, first_moment, second_moment))
    averaged = lax.optimization_barrier(jnp.sum(pseudo_grads, axis=0)) / N_REPLICA
    new_anchor, new_momentum = outer_step(averaged, outer_momentum, anchor)
    return (new_weight, new_first, new_second, new_anchor, new_momentum)
```

```python
import functools

import jax
import jax.numpy as jnp
from jax import lax
from jax.experimental import pallas as pl
from jax.experimental.pallas import tpu as pltpu
from jax.sharding import PartitionSpec as P

HD = 128
STEP = 5
RING = 4

first_decay = 0.9
second_decay = 0.95
inner_rate = 0.001
weight_decay = 0.1
adam_epsilon = 1e-08
outer_rate = 0.7
outer_decay = 0.9


def attention_grads(query_rows, grad_rows, key_rows, value_rows):
    length = key_rows.shape[0]
    kv_heads = key_rows.shape[1] // HD
    members = query_rows.shape[1] // key_rows.shape[1]
    scaling = HD ** (-0.5)
    query_heads = query_rows.reshape(length, kv_heads, members, HD)
    grad_heads = grad_rows.reshape(length, kv_heads, members, HD)
    key_heads = key_rows.reshape(length, kv_heads, HD)
    value_heads = value_rows.reshape(length, kv_heads, HD)
    scores = (
        jnp.einsum("ihgd,jhd->hgij", query_heads, key_heads, preferred_element_type=jnp.float32)
        * scaling
    )
    causal = jnp.arange(length)[:, None] >= jnp.arange(length)[None, :]
    scores = jnp.where(causal, scores, -jnp.inf)
    probabilities = jax.nn.softmax(scores, axis=-1)
    rounded_probs = probabilities.astype(jnp.bfloat16)
    value_grads = jnp.einsum(
        "hgij,ihgd->jhd", rounded_probs, grad_heads, preferred_element_type=jnp.float32
    )
    prob_grads = jnp.einsum(
        "ihgd,jhd->hgij", grad_heads, value_heads, preferred_element_type=jnp.float32
    )
    row_delta = jnp.sum(probabilities * prob_grads, axis=-1, keepdims=True)
    score_grads = (probabilities * (prob_grads - row_delta) * scaling).astype(jnp.bfloat16)
    key_grads = jnp.einsum(
        "hgij,ihgd->jhd", score_grads, query_heads, preferred_element_type=jnp.float32
    )
    joined = jnp.concatenate(
        [key_grads.reshape(length, -1), value_grads.reshape(length, -1)], axis=1
    )
    return joined.astype(jnp.bfloat16)


def apply_adamw(weights, first_moment, second_moment, gradient):
    first_new = first_decay * first_moment.astype(jnp.float32) + (1.0 - first_decay) * gradient
    second_new = (
        second_decay * second_moment.astype(jnp.float32)
        + (1.0 - second_decay) * gradient * gradient
    )
    corrected_first = first_new / (1.0 - first_decay**STEP)
    corrected_second = second_new / (1.0 - second_decay**STEP)
    current = weights.astype(jnp.float32)
    updated = current - inner_rate * (
        corrected_first / (jnp.sqrt(corrected_second) + adam_epsilon) + weight_decay * current
    )
    return (
        updated.astype(jnp.bfloat16),
        first_new.astype(jnp.bfloat16),
        second_new.astype(jnp.bfloat16),
    )


def outer_step(averaged, momentum, anchor):
    momentum_new = outer_decay * momentum + averaged
    anchor_new = anchor - outer_rate * (averaged + outer_decay * momentum_new)
    return (anchor_new, momentum_new)


def place():
    f, t = lax.axis_index("fsdp"), lax.axis_index("tensor")
    return f, t, f // RING, f % RING, t // 2, t % 2


def at(z_low, y, z_high, core):
    return {"fsdp": z_low * RING + y, "tensor": z_high * 2 + core}


def send(src, dst, sems, slot, where):
    return pltpu.make_async_remote_copy(
        src_ref=src,
        dst_ref=dst,
        send_sem=sems[0].at[slot],
        recv_sem=sems[1].at[slot],
        device_id=where,
        device_id_type=pl.DeviceIdType.MESH,
    )


def greet(partners):
    barrier = pltpu.get_barrier_semaphore()
    for partner in partners:
        pl.semaphore_signal(
            barrier, inc=1, device_id=partner, device_id_type=pl.DeviceIdType.MESH
        )
    pl.semaphore_wait(barrier, len(partners))


def gather_kernel(
    tok_ref, w_ref, tok_all, kv_ref, w_all, t_send, t_recv, l_send, l_recv, y_send, y_recv
):
    f, t, zl, y, zh, c = place()
    up, down = at(zl, y, (zh + 1) % RING, c), at(zl, y, (zh + 3) % RING, c)
    sibling = at(zl, y, zh, 1 - c)
    right, left = at(zl, (y + 1) % RING, zh, c), at(zl, (y + 3) % RING, zh, c)
    line = [at((zl + k) % RING, y, zh, c) for k in range(1, RING)]
    greet([up, down, sibling, right, left] + line)

    rows = tok_ref.shape[0]
    half = rows // 2
    top, bottom = pl.ds(0, half), pl.ds(half, half)
    t_below = (zh + 3) % RING * 2 + c
    t_above = (zh + 1) % RING * 2 + c
    t_far = (zh + 2) % RING * 2 + c
    flip = 1 - 2 * c
    ts, ls, ys = (t_send, t_recv), (l_send, l_recv), (y_send, y_recv)
    started = []

    def go(copy):
        copy.start()
        started.append(copy)

    for k in range(1, RING):
        go(send(w_ref, w_all.at[f], ls, k - 1, line[k - 1]))
    go(send(w_ref, w_all.at[f], ys, 0, right))
    go(send(w_ref, w_all.at[f], ys, 1, left))
    go(send(tok_ref, tok_all.at[t], ts, 0, up))
    go(send(tok_ref, tok_all.at[t], ts, 1, down))
    go(send(tok_ref, tok_all.at[t], ts, 2, sibling))
    tok_all[t] = tok_ref[...]
    w_all[f] = w_ref[...]

    def arrived(ref, sems, slot):
        send(ref, ref, sems, slot, sibling).wait_recv()

    def pass_on(k):
        z_from = (zl + RING - k) % RING
        from_left = z_from * RING + (y + 3) % RING
        from_right = z_from * RING + (y + 1) % RING
        arrived(w_all.at[from_left], ys, 4 * k)
        go(send(w_all.at[from_left, 0], w_all.at[from_left, 0], ys, 4 * k + 2, right))
        arrived(w_all.at[from_right], ys, 4 * k + 1)
        go(send(w_all.at[from_right, 1], w_all.at[from_right, 1], ys, 4 * k + 3, left))

    for k in range(1, RING):
        mine = (zl + RING - k) % RING * RING + y
        arrived(w_all.at[mine], ls, k - 1)
        go(send(w_all.at[mine], w_all.at[mine], ys, 4 * k, right))
        go(send(w_all.at[mine], w_all.at[mine], ys, 4 * k + 1, left))
        pass_on(k - 1)

    arrived(tok_all.at[t_below], ts, 0)
    go(send(tok_all.at[t_below, top], tok_all.at[t_below, top], ts, 3, up))
    go(send(tok_all.at[t_below], tok_all.at[t_below], ts, 5, sibling))
    arrived(tok_all.at[t_above], ts, 1)
    go(send(tok_all.at[t_above, bottom], tok_all.at[t_above, bottom], ts, 4, down))
    go(send(tok_all.at[t_above], tok_all.at[t_above], ts, 6, sibling))
    pass_on(RING - 1)
    for k in range(RING):
        opposite = (zl + RING - k) % RING * RING + (y + 2) % RING
        arrived(w_all.at[opposite, 0], ys, 4 * k + 2)
        arrived(w_all.at[opposite, 1], ys, 4 * k + 3)

    def term(block):
        pair = w_all[pl.ds(2 * block, 2)]
        piece = tok_all[block]
        return [
            jnp.dot(
                piece,
                pair[:, i].reshape(-1, pair.shape[-1]),
                preferred_element_type=jnp.float32,
            )
            for i in range(2)
        ]

    def plus(a, b):
        return [p + q for p, q in zip(a, b)]

    total = term(t)
    total = plus(total, term(t_below))
    total = plus(total, term(t_above))
    arrived(tok_all.at[t + flip], ts, 2)
    total = plus(total, term(t + flip))
    arrived(tok_all.at[t_below + flip], ts, 5)
    total = plus(total, term(t_below + flip))
    arrived(tok_all.at[t_above + flip], ts, 6)
    total = plus(total, term(t_above + flip))
    arrived(tok_all.at[t_far, top], ts, 3)
    go(send(tok_all.at[t_far, top], tok_all.at[t_far, top], ts, 7, sibling))
    arrived(tok_all.at[t_far, bottom], ts, 4)
    go(send(tok_all.at[t_far, bottom], tok_all.at[t_far, bottom], ts, 8, sibling))
    total = plus(total, term(t_far))
    arrived(tok_all.at[t_far + flip, top], ts, 7)
    arrived(tok_all.at[t_far + flip, bottom], ts, 8)
    total = plus(total, term(t_far + flip))
    kv_ref[0] = total[0].astype(kv_ref.dtype)
    kv_ref[1] = total[1].astype(kv_ref.dtype)
    for copy in started:
        copy.wait_send()


def scatter_kernel(
    tok_all, grad_ref, out_ref, term, first, second, done, landed,
    f_send, f_recv, s_send, s_recv, l_send, l_recv,
):
    f, t, zl, y, zh, c = place()
    right, left = at(zl, (y + 1) % RING, zh, c), at(zl, (y + 3) % RING, zh, c)
    line = [at((zl + k) % RING, y, zh, c) for k in range(1, RING)]
    greet([right, left] + line)

    fs, ss, ls = (f_send, f_recv), (s_send, s_recv), (l_send, l_recv)
    width = out_ref.shape[1]
    half = out_ref.shape[0] // 2
    top, bottom = pl.ds(0, half), pl.ds(half, half)
    grads = grad_ref[...]
    started = []

    def go(copy):
        copy.start()
        started.append(copy)

    def make(z_to, y_to, slot):
        block = z_to * RING + y_to
        piece = tok_all[block // 2, :, pl.ds(pl.multiple_of(block % 2 * width, width), width)]
        term[slot] = jnp.dot(grads, piece, preferred_element_type=jnp.float32).astype(term.dtype)

    order = [1, 2, 3, 0]
    for n, k in enumerate(order):
        make((zl + k) % RING, (y + 2) % RING, 4 * n + 2)
        go(send(term.at[4 * n + 2, top], first.at[n, top], fs, 2 * n, right))
        go(send(term.at[4 * n + 2, bottom], first.at[n, bottom], fs, 2 * n + 1, left))
    for n, k in enumerate(order):
        z_to = (zl + k) % RING
        make(z_to, (y + 1) % RING, 4 * n + 1)
        make(z_to, (y + 3) % RING, 4 * n + 3)
        make(z_to, y, 4 * n)

    def arrived(ref, sems, slot):
        send(ref, ref, sems, slot, right).wait_recv()

    def add(slot, part, other):
        term[slot, part] = (
            term[slot, part].astype(jnp.float32) + other.astype(jnp.float32)
        ).astype(term.dtype)

    def middle(n):
        arrived(first.at[n, top], fs, 2 * n)
        add(4 * n + 1, top, first[n, top])
        go(send(term.at[4 * n + 1], second.at[n, 0], ss, 2 * n, right))
        arrived(first.at[n, bottom], fs, 2 * n + 1)
        add(4 * n + 3, bottom, first[n, bottom])
        go(send(term.at[4 * n + 3], second.at[n, 1], ss, 2 * n + 1, left))

    def finish(n):
        arrived(second.at[n, 0], ss, 2 * n)
        arrived(second.at[n, 1], ss, 2 * n + 1)
        total = (
            term[4 * n].astype(jnp.float32)
            + second[n, 0].astype(jnp.float32)
            + second[n, 1].astype(jnp.float32)
        )
        k = order[n]
        if k:
            done[n] = total.astype(done.dtype)
            go(send(done.at[n], landed.at[n], ls, n, line[k - 1]))
        else:
            out_ref[...] = total

    middle(0)
    for n in range(RING):
        if n + 1 < RING:
            middle(n + 1)
        finish(n)
    for n in range(RING - 1):
        arrived(landed.at[n], ls, n)
        out_ref[...] += landed[n].astype(jnp.float32)
    for copy in started:
        copy.wait_send()


def gather(tokens, weights):
    rows, depth = tokens.shape
    vmem = pl.BlockSpec(memory_space=pltpu.VMEM)
    sems = pltpu.SemaphoreType.DMA
    return pl.pallas_call(
        gather_kernel,
        out_shape=(
            jax.ShapeDtypeStruct((8, rows, depth), jnp.bfloat16),
            jax.ShapeDtypeStruct((2, rows, HD), jnp.bfloat16),
        ),
        in_specs=[vmem] * 2,
        out_specs=(vmem, vmem),
        scratch_shapes=[
            pltpu.VMEM((16,) + weights.shape, jnp.bfloat16),
            sems((9,)), sems((9,)),
            sems((3,)), sems((3,)),
            sems((16,)), sems((16,)),
        ],
        compiler_params=pltpu.CompilerParams(
            collective_id=0, has_side_effects=True, vmem_limit_bytes=48 * 2**20
        ),
        name="gather_project",
    )(tokens, weights)


def scatter(tok_all, grads_t, width):
    features = grads_t.shape[0]
    vmem = pl.BlockSpec(memory_space=pltpu.VMEM)
    sems = pltpu.SemaphoreType.DMA
    block = (features, width)
    return pl.pallas_call(
        scatter_kernel,
        out_shape=jax.ShapeDtypeStruct(block, jnp.float32),
        in_specs=[vmem] * 2,
        out_specs=vmem,
        scratch_shapes=[
            pltpu.VMEM((16,) + block, jnp.bfloat16),
            pltpu.VMEM((4,) + block, jnp.bfloat16),
            pltpu.VMEM((4, 2) + block, jnp.bfloat16),
            pltpu.VMEM((3,) + block, jnp.bfloat16),
            pltpu.VMEM((3,) + block, jnp.bfloat16),
            sems((8,)), sems((8,)),
            sems((8,)), sems((8,)),
            sems((3,)), sems((3,)),
        ],
        compiler_params=pltpu.CompilerParams(
            collective_id=1, has_side_effects=True, vmem_limit_bytes=48 * 2**20
        ),
        name="gradient_scatter",
    )(tok_all, grads_t)


def shards(
    tokens,
    queries,
    out_grad,
    kv_weight,
    first_moment,
    second_moment,
    pseudo_grads,
    outer_momentum,
    anchor,
):
    weights = kv_weight[0]
    own_term = pseudo_grads[0]
    replicas = lax.axis_size("replica")
    averaged = lax.psum(own_term.astype(jnp.bfloat16), "replica").astype(jnp.float32) / replicas
    new_anchor, new_momentum = outer_step(averaged, outer_momentum, anchor)

    tok_all, kv = gather(tokens[0], weights)
    kv_grads = attention_grads(queries[0], out_grad[0], kv[0], kv[1])
    summed = scatter(tok_all, kv_grads.T, weights.shape[1])
    gradient = summed.reshape(2, HD, weights.shape[1]).transpose(0, 2, 1)
    new_weight, new_first, new_second = apply_adamw(
        weights, first_moment[0], second_moment[0], gradient
    )
    return (new_weight[None], new_first[None], new_second[None], new_anchor, new_momentum)


def solution(mesh):
    return jax.shard_map(
        shards,
        mesh=mesh,
        in_specs=(
            P("replica", "fsdp", "tensor"),
            P("replica", "fsdp", "tensor"),
            P("replica", "fsdp", "tensor"),
            P("replica", None, "fsdp", "tensor"),
            P("replica", None, "fsdp", "tensor"),
            P("replica", None, "fsdp", "tensor"),
            P("replica", "fsdp", "tensor"),
            P("fsdp", "tensor"),
            P("fsdp", "tensor"),
        ),
        out_specs=(
            P("replica", None, "fsdp", "tensor"),
            P("replica", None, "fsdp", "tensor"),
            P("replica", None, "fsdp", "tensor"),
            P("fsdp", "tensor"),
            P("fsdp", "tensor"),
        ),
        check_vma=False,
    )
```
